32 devices in a mesh: var: 4 (over z), own: 4 (over y, x), sub: 2 (over core).
Axes of the slice: x: 2, y: 2, z: 4, core: 2. Of those that a mesh axis runs over, the one named last changes fastest.
Arguments:
- capacity_blocks: bfloat16 [2048, 5, 128, 128], P(('var', 'own', 'sub')), may hold values from -0.078125 to 0.078125
- capacity_rows: int32 [2048, 5], P(('var', 'own', 'sub')), may hold values from 0 to 7, all different within a row
- cover_self: bfloat16 [2048, 128, 128], P(('var', 'own', 'sub')), may hold values from -0.5 to 0.5
- cover_prev: bfloat16 [2048, 128, 128], P(('var', 'own', 'sub')), may hold values from -0.5 to 0.5
- scaling: bfloat16 [2048, 128], P(('var', 'own', 'sub')), may hold values from 0.099609375 to 10
Outputs:
- cover_diag: bfloat16 [2048, 128, 128], P(('var', 'own', 'sub'))
- cover_lower: bfloat16 [2048, 128, 128], P(('var', 'own', 'sub'))
- capacity_normal: float32 [1024, 1024], P(('var', 'own', 'sub'))
The draws below stay inside these ranges and needn't reach their ends.
Inputs may be any that keep to these rules, and one draw needn't show every extreme that they name: `capacity_rows`: each column block names 5 different capacity row blocks, and every capacity row block is named somewhere.
All inputs are finite; a program needn't handle non-finite values.
Results may differ from the reference program's by a relative error of at most 0.0049.
Values may be sent and summed in bfloat16 or wider, within the bound.
No kernel may reach another device: no remote copies, remote signals or barrier semaphores. Data moves between devices by JAX's collectives and lax.ppermute only.
A program may use at most 192 MiB of HBM per device.

```python
import math
import jax
import jax.numpy as jnp
from jax import lax

BLK = 128
NZ = 5
CAP = 8
CB_DEV = 64
NCB = 2048
DEVICES = 32


def steps_of(stream_key, dims, cuts, low, high):
    def one(axis_at, blocks):
        draws = jax.random.uniform(jax.random.fold_in(jax.random.fold_in(stream_key, 6), axis_at), (blocks,), jnp.float32, low / len(cuts), high / len(cuts))
        return jnp.repeat(jnp.exp(draws), dims[axis_at] // blocks).reshape((-1,) + (1,) * (len(dims) - axis_at - 1))

    loudness = one(*cuts[0])
    for cut in cuts[1:]:
        loudness = loudness * one(*cut)
    return loudness


def picks_of(stream_key, rows, count, top, lift):
    ranking = jax.random.permutation(jax.random.fold_in(stream_key, 1), count)
    pull = ranking
    for power in range(3):
        pull = pull * pull // count
    pull = pull * lift // count
    tickets = jax.random.randint(jax.random.fold_in(stream_key, 2), (rows, count), 0, 4096) + pull
    fixed_rows = jax.random.permutation(jax.random.fold_in(stream_key, 3), rows)[jnp.arange(count) % rows]
    tickets = jnp.where(jnp.arange(rows)[:, None] == fixed_rows[None, :], 1 << 14, tickets)
    merit = tickets * count + jnp.arange(count)
    return lax.top_k(merit.astype(jnp.int32), top)[1].astype(jnp.int32)


def scatter_about(own_key, dims, deviation, reach, shards=(), dtype=jnp.bfloat16):
    entries = jax.random.normal(own_key, dims, jnp.float32) * deviation
    if len(shards) > 0:
        entries = steps_of(own_key, dims, shards, -0.22, 0.18) * entries
    return jnp.clip(entries, min=-reach, max=reach).astype(dtype)


def setup_inputs(seed: int = 0) -> dict:
    splits = jax.random.split(jax.random.key(seed), 6)
    return {
        "capacity_blocks": scatter_about(splits[0], (NCB, NZ, BLK, BLK), (CB_DEV * DEVICES * NZ * BLK // (CAP * 32)) ** -0.5, 0.078125, ((0, 32),)),
        "capacity_rows": picks_of(splits[1], NCB, CAP, NZ, 10240),
        "cover_self": scatter_about(splits[2], (NCB, BLK, BLK), BLK ** -0.5, 0.5, ((0, 32),)),
        "cover_prev": scatter_about(splits[3], (NCB, BLK, BLK), BLK ** -0.5, 0.5, ((0, 32),)),
        "scaling": jnp.clip(jnp.exp(math.log(10.0) - 4.609084 * jax.random.uniform(splits[4], (NCB, BLK), jnp.float32) ** steps_of(splits[4], (NCB, BLK), ((0, 32),), -0.2, 0.2)), 0.099609375, 10.0).astype(jnp.bfloat16),
    }


def accumulate(partial_value, inputs):
    blocks, row_ids, scale_row = inputs
    scaled = (blocks.astype(jnp.float32) * scale_row.astype(jnp.float32)[:, None, None, :]).astype(jnp.bfloat16)
    tile_sums = jnp.einsum("kpiv,kqjv->kpqij", scaled.astype(jnp.float32), blocks.astype(jnp.float32))
    per_block = row_ids.shape[1]
    left_rows = jnp.broadcast_to(row_ids[:, :, None], (row_ids.shape[0], per_block, per_block)).reshape(-1)
    right_rows = jnp.broadcast_to(row_ids[:, None, :], (row_ids.shape[0], per_block, per_block)).reshape(-1)
    edge_size = blocks.shape[-1]
    partial_value = partial_value.at[left_rows, :, right_rows, :].add(tile_sums.reshape(-1, edge_size, edge_size))
    return partial_value, None


def reference(capacity_blocks, capacity_rows, cover_self, cover_prev, scaling):
    total_blocks = capacity_blocks.shape[0]
    group_size = math.gcd(total_blocks, 64)
    turns = total_blocks // group_size
    inputs = (capacity_blocks.reshape((turns, group_size) + capacity_blocks.shape[1:]),
              capacity_rows.reshape(turns, group_size, -1),
              scaling.reshape(turns, group_size, -1))
    start = jnp.zeros((CAP, BLK, CAP, BLK), jnp.float32)
    result, unused = lax.scan(accumulate, start, inputs)
    capacity_normal = result.reshape(CAP * BLK, CAP * BLK)
    scaled_self = (cover_self.astype(jnp.float32) * scaling.astype(jnp.float32)[:, None, :]).astype(jnp.bfloat16)
    scale_prev = jnp.concatenate([jnp.zeros((1, BLK), jnp.bfloat16), scaling[:-1]], axis=0)
    self_prev = jnp.concatenate([jnp.zeros((1, BLK, BLK), jnp.bfloat16), cover_self[:-1]], axis=0)
    scaled_prev = (cover_prev.astype(jnp.float32) * scale_prev.astype(jnp.float32)[:, None, :]).astype(jnp.bfloat16)
    diag_sum = jnp.einsum("kiv,kjv->kij", scaled_self.astype(jnp.float32), cover_self.astype(jnp.float32))
    diag_sum = diag_sum + jnp.einsum("kiv,kjv->kij", scaled_prev.astype(jnp.float32), cover_prev.astype(jnp.float32))
    lower_sum = jnp.einsum("kiv,kjv->kij", scaled_prev.astype(jnp.float32), self_prev.astype(jnp.float32))
    return diag_sum.astype(jnp.bfloat16), lower_sum.astype(jnp.bfloat16), capacity_normal
```

```python
import functools

import jax
import jax.numpy as jnp
from jax import lax
from jax.experimental import pallas as pl
from jax.experimental.pallas import tpu as pltpu
from jax.sharding import PartitionSpec as P

CAP = 8
AXES = ("var", "own", "sub")
NT = (((1,), (1,)), ((), ()))
F32, BF16 = jnp.float32, jnp.bfloat16


def swap(value, axis, mask):
    count = lax.axis_size(axis)
    return lax.ppermute(value, axis, [(i, i ^ mask) for i in range(count)])


def shifted(value, axis, steps):
    count = lax.axis_size(axis)
    return lax.ppermute(value, axis, [(i, i + steps) for i in range(count - steps)])


def set_bits(mask, count):
    found = []
    for _ in range(count):
        low = mask & (-mask)
        found.append(
            jnp.where((low & 0xAA) != 0, 1, 0)
            + jnp.where((low & 0xCC) != 0, 2, 0)
            + jnp.where((low & 0xF0) != 0, 4, 0)
        )
        mask = mask ^ low
    return found


def capacity_kernel(step, parts, sizes, rows_ref, place_ref, cap_ref, scale_ref, *rest):
    outs, (dense, scale, acc, sems) = rest[: 2 * len(parts)], rest[2 * len(parts) :]
    count, width = cap_ref.shape[0], cap_ref.shape[2]
    nz = cap_ref.shape[1] // width
    turns = count // step
    side = acc.shape[0]
    tile = 2 * width

    def spot(r):
        return pl.ds(pl.multiple_of(r * width, width), width)

    def issue(k, carry):
        for p in range(nz):
            pltpu.make_async_copy(
                cap_ref.at[k, pl.ds(p * width, width), :],
                dense.at[k, spot(rows_ref[p, k]), :],
                sems.at[k // step],
            ).start()
        return carry

    def clear(k):
        mask = jnp.int32(0)
        for p in range(nz):
            mask = mask | jnp.left_shift(jnp.int32(1), rows_ref[p, k])
        for r in set_bits((1 << CAP) - 1 - mask, CAP - nz):
            dense[k, spot(r), :] = jnp.zeros((width, width), BF16)

    lax.fori_loop(0, step, issue, 0)
    scale[...] = scale_ref[...].astype(F32)
    for k in range(step):
        clear(k)
    lax.fori_loop(step, count, issue, 0)
    acc[...] = jnp.zeros_like(acc)

    def turn(t, carry):
        first = t * step
        pltpu.make_async_copy(
            cap_ref.at[pl.ds(first, step)],
            dense.at[pl.ds(first, step), pl.ds(0, nz * width), :],
            sems.at[t],
        ).wait()
        following = jnp.minimum(t + 1, turns - 1) * step
        for i in range(step):
            clear(following + i)
        ks = [first + i for i in range(step)]
        for j in range(side // tile):
            right = jnp.concatenate(
                [dense[k, pl.ds(tile * j, tile), :] * scale[pl.ds(k, 1), :].astype(BF16) for k in ks], axis=1
            )
            left = jnp.concatenate([dense[k, pl.ds(0, tile * (j + 1)), :] for k in ks], axis=1)
            acc[pl.ds(0, tile * (j + 1)), pl.ds(tile * j, tile)] += lax.dot_general(
                left, right, NT, preferred_element_type=F32
            )
        return carry

    lax.fori_loop(0, turns, turn, 0)
    for i in range(side // tile):
        for j in range(i):
            acc[pl.ds(tile * i, tile), pl.ds(tile * j, tile)] = acc[pl.ds(tile * j, tile), pl.ds(tile * i, tile)].T
    var, own, sub = place_ref[0], place_ref[1], place_ref[2]
    n_var, n_own, held = sizes
    for at, (low, high, order) in enumerate(parts):
        keep_ref, send_ref = outs[2 * at], outs[2 * at + 1]
        for slot, m in enumerate(order):

            def emit(v, carry):
                chip = (var ^ v) * n_own + (own ^ m)
                mine = pl.ds(pl.multiple_of((2 * chip + sub) * held, held), held)
                other = pl.ds(pl.multiple_of((2 * chip + 1 - sub) * held, held), held)
                keep_ref[slot, v] = acc[mine, pl.ds(low, high - low)]
                send_ref[slot, v] = acc[other, pl.ds(low, high - low)].astype(send_ref.dtype)
                return carry

            lax.fori_loop(0, n_var, emit, 0)


def capacity(capacity_blocks, capacity_rows, scaling, parts):
    count, nz, width = capacity_blocks.shape[:3]
    n_var, n_own, n_sub = (lax.axis_size(a) for a in AXES)
    side = CAP * width
    held = side // (n_var * n_own * n_sub)
    step = 16
    place = jnp.stack([lax.axis_index(a) for a in AXES]).astype(jnp.int32)
    sent = BF16 if held % 16 == 0 else F32
    shapes = []
    for low, high, _ in parts:
        shapes += [
            jax.ShapeDtypeStruct((n_own, n_var, held, high - low), F32),
            jax.ShapeDtypeStruct((n_own, n_var, held, high - low), sent),
        ]
    smem, vmem = pl.BlockSpec(memory_space=pltpu.SMEM), pl.BlockSpec(memory_space=pltpu.VMEM)
    flops = 2 * side * side * count * width * 5 // 8
    outs = pl.pallas_call(
        functools.partial(capacity_kernel, step, parts, (n_var, n_own, held)),
        out_shape=shapes,
        in_specs=[smem, smem, pl.BlockSpec(memory_space=pltpu.HBM), vmem],
        out_specs=[vmem] * len(shapes),
        scratch_shapes=[
            pltpu.VMEM((count, side, width), BF16),
            pltpu.VMEM((count, width), F32),
            pltpu.VMEM((side, side), F32),
            pltpu.SemaphoreType.DMA((count // step,)),
        ],
        compiler_params=pltpu.CompilerParams(vmem_limit_bytes=54 * 2**20),
        cost_estimate=pl.CostEstimate(flops=flops, bytes_accessed=14 * 2**20, transcendentals=0),
        name="capacity",
    )(capacity_rows.T, place, capacity_blocks.reshape(count, nz * width, width), scaling)
    return [(keep, send.astype(BF16)) for keep, send in zip(outs[0::2], outs[1::2])]


def cover_kernel(self_ref, before_ref, prev_ref, scale_ref, got_self_ref, got_scale_ref, diag_ref, lower_ref, scale):
    group = self_ref.shape[0]
    at = pl.program_id(0)

    @pl.when(at == 0)
    def _():
        scale[pl.ds(0, 1), :] = got_scale_ref[...].astype(F32)
        scale[pl.ds(8, scale_ref.shape[0]), :] = scale_ref[...].astype(F32)

    base = 8 + at * group
    for k in range(group):
        mine = self_ref[k]
        prev = prev_ref[k]
        if k == 0:
            before = jnp.where(at == 0, got_self_ref[0], before_ref[0])
            scale_before = scale[pl.ds(jnp.where(at == 0, 0, base - 1), 1), :]
        else:
            before = self_ref[k - 1]
            scale_before = scale[pl.ds(base + k - 1, 1), :]
        left = jnp.concatenate(
            [mine * scale[pl.ds(base + k, 1), :].astype(BF16), prev * scale_before.astype(BF16)], axis=1
        )
        right = jnp.concatenate(
            [
                jnp.concatenate([mine, prev], axis=1),
                jnp.concatenate([jnp.zeros_like(before), before], axis=1),
            ],
            axis=0,
        )
        both = lax.dot_general(left, right, NT, preferred_element_type=F32)
        width = mine.shape[0]
        diag_ref[k] = both[:, :width].astype(BF16)
        lower_ref[k] = both[:, width:].astype(BF16)


def cover(cover_self, cover_prev, scaling, got_self, got_scale):
    count, width = cover_self.shape[:2]
    group = 16
    block = pl.BlockSpec((group, width, width), lambda i: (i, 0, 0))
    whole = pl.BlockSpec(memory_space=pltpu.VMEM)
    return pl.pallas_call(
        cover_kernel,
        grid=(count // group,),
        out_shape=[jax.ShapeDtypeStruct(cover_self.shape, BF16)] * 2,
        in_specs=[
            block,
            pl.BlockSpec((1, width, width), lambda i: (jnp.maximum(i * group - 1, 0), 0, 0)),
            block,
            whole,
            whole,
            whole,
        ],
        out_specs=[block, block],
        scratch_shapes=[pltpu.VMEM((8 + count, width), F32)],
        compiler_params=pltpu.CompilerParams(vmem_limit_bytes=16 * 2**20),
        cost_estimate=pl.CostEstimate(
            flops=2 * count * width * 4 * width * width, bytes_accessed=4 * 2 * count * width * width, transcendentals=0
        ),
        name="cover",
    )(cover_self, cover_self, cover_prev, scaling, got_self, got_scale)


def body(capacity_blocks, capacity_rows, cover_self, cover_prev, scaling):
    n_var, n_own, n_sub = (lax.axis_size(a) for a in AXES)
    got_self = shifted(cover_self[-1:], AXES, 1)
    got_scale = shifted(scaling[-1:], AXES, 1)
    side = CAP * capacity_blocks.shape[2]
    ((keep, send),) = capacity(capacity_blocks, capacity_rows, scaling, ((0, side, tuple(range(n_own))),))
    total = keep + swap(send, "sub", 1).astype(F32)
    for axis in ("own", "var"):
        masks = range(1, lax.axis_size(axis))
        arrived = [swap(total[m].astype(BF16), axis, m) for m in masks]
        total = total[0]
        for term in arrived:
            total = total + term.astype(F32)
    diag, lower = cover(cover_self, cover_prev, scaling, got_self, got_scale)
    return (diag, lower, total)


def solution(mesh):
    split = P(AXES)
    return jax.shard_map(
        body, mesh=mesh, in_specs=(split,) * 5, out_specs=(split,) * 3, check_vma=False
    )
```

```python
import functools

import jax
import jax.numpy as jnp
from jax import lax
from jax.experimental import pallas as pl
from jax.experimental.pallas import tpu as pltpu
from jax.sharding import PartitionSpec as P

CAP = 8
AXES = ("var", "own", "sub")
NT = (((1,), (1,)), ((), ()))
F32, BF16 = jnp.float32, jnp.bfloat16


def swap(value, axis, mask):
    count = lax.axis_size(axis)
    return lax.ppermute(value, axis, [(i, i ^ mask) for i in range(count)])


def shifted(value, axis, steps):
    count = lax.axis_size(axis)
    return lax.ppermute(value, axis, [(i, i + steps) for i in range(count - steps)])


def send_order(axis):
    masks = list(range(1, lax.axis_size(axis)))
    return masks[1:] + masks[:1] if axis == "var" else masks[::-1]


def set_bits(mask, count):
    found = []
    for _ in range(count):
        low = mask & (-mask)
        found.append(
            jnp.where((low & 0xAA) != 0, 1, 0)
            + jnp.where((low & 0xCC) != 0, 2, 0)
            + jnp.where((low & 0xF0) != 0, 4, 0)
        )
        mask = mask ^ low
    return found


def capacity_kernel(step, parts, sizes, rows_ref, cap_ref, scale_ref, *rest):
    outs, (dense, scale_in, scale, acc, sems, scale_sem) = rest[: 2 * len(parts)], rest[2 * len(parts) :]
    count, width = cap_ref.shape[0], cap_ref.shape[2]
    nz = cap_ref.shape[1] // width
    turns = count // step
    side = acc.shape[0]
    tile = 2 * width

    def spot(r):
        return pl.ds(pl.multiple_of(r * width, width), width)

    def lay(k, carry):
        mask = jnp.int32(0)
        for p in range(nz):
            r = rows_ref[p, k]
            mask = mask | jnp.left_shift(jnp.int32(1), r)
            pltpu.make_async_copy(
                cap_ref.at[k, pl.ds(p * width, width), :], dense.at[k, spot(r), :], sems.at[k // step]
            ).start()
        for r in set_bits((1 << CAP) - 1 - mask, CAP - nz):
            dense[k, spot(r), :] = jnp.zeros((width, width), BF16)
        return carry

    fetch = pltpu.make_async_copy(scale_ref, scale_in, scale_sem)
    fetch.start()
    lax.fori_loop(0, count, lay, 0, unroll=4)
    fetch.wait()
    scale[...] = scale_in[...].astype(F32)
    acc[...] = jnp.zeros_like(acc)

    def turn(t, carry):
        first = t * step
        pltpu.make_async_copy(
            cap_ref.at[pl.ds(first, step)],
            dense.at[pl.ds(first, step), pl.ds(0, nz * width), :],
            sems.at[t],
        ).wait()
        ks = [first + i for i in range(step)]
        for j in range(side // tile):
            right = jnp.concatenate(
                [dense[k, pl.ds(tile * j, tile), :] * scale[pl.ds(k, 1), :].astype(BF16) for k in ks], axis=1
            )
            left = jnp.concatenate([dense[k, pl.ds(0, tile * (j + 1)), :] for k in ks], axis=1)
            acc[pl.ds(0, tile * (j + 1)), pl.ds(tile * j, tile)] += lax.dot_general(
                left, right, NT, preferred_element_type=F32
            )
        return carry

    lax.fori_loop(0, turns, turn, 0)
    for i in range(side // tile):
        for j in range(i):
            acc[pl.ds(tile * i, tile), pl.ds(tile * j, tile)] = acc[pl.ds(tile * j, tile), pl.ds(tile * i, tile)].T
    var, own, sub = (lax.axis_index(a) for a in AXES)
    n_var, n_own, held = sizes
    for at, (low, high, first) in enumerate(parts):
        keep_ref, send_ref = outs[2 * at], outs[2 * at + 1]
        for m in range(n_own):

            def emit(v, carry, m=m):
                chip = (var ^ v) * n_own + (own ^ m)
                mine = pl.ds(pl.multiple_of((2 * chip + sub) * held, held), held)
                other = pl.ds(pl.multiple_of((2 * chip + 1 - sub) * held, held), held)
                slot = (m, v) if first == "own" else (v, m)
                keep_ref[slot] = acc[mine, pl.ds(low, high - low)]
                send_ref[slot] = acc[other, pl.ds(low, high - low)].astype(send_ref.dtype)
                return carry

            lax.fori_loop(0, n_var, emit, 0)


def capacity(capacity_blocks, capacity_rows, scaling, parts):
    count, nz, width = capacity_blocks.shape[:3]
    n_var, n_own, n_sub = (lax.axis_size(a) for a in AXES)
    side = CAP * width
    held = side // (n_var * n_own * n_sub)
    step = 16
    sent = BF16 if held % 16 == 0 else F32
    shapes = []
    for low, high, first in parts:
        lead = (n_own, n_var) if first == "own" else (n_var, n_own)
        shapes += [jax.ShapeDtypeStruct(lead + (held, high - low), t) for t in (F32, sent)]
    hbm = pl.BlockSpec(memory_space=pltpu.HBM)
    smem, vmem = pl.BlockSpec(memory_space=pltpu.SMEM), pl.BlockSpec(memory_space=pltpu.VMEM)
    operands = (capacity_rows.T, capacity_blocks.reshape(count, nz * width, width), scaling)
    flops = 2 * side * side * count * width * 5 // 8
    outs = pl.pallas_call(
        functools.partial(capacity_kernel, step, parts, (n_var, n_own, held)),
        out_shape=shapes,
        in_specs=[smem, hbm, hbm],
        out_specs=[vmem] * len(shapes),
        scratch_shapes=[
            pltpu.VMEM((count, side, width), BF16),
            pltpu.VMEM((count, width), BF16),
            pltpu.VMEM((count, width), F32),
            pltpu.VMEM((side, side), F32),
            pltpu.SemaphoreType.DMA((count // step,)),
            pltpu.SemaphoreType.DMA,
        ],
        compiler_params=pltpu.CompilerParams(vmem_limit_bytes=32 * 2**20),
        cost_estimate=pl.CostEstimate(flops=flops, bytes_accessed=14 * 2**20, transcendentals=0),
        name="capacity",
    )(*(pltpu.with_memory_space_constraint(x, pltpu.HBM) for x in operands))
    return [(keep, send.astype(BF16)) for keep, send in zip(outs[0::2], outs[1::2])]


def cover_kernel(group, self_ref, prev_ref, scale_ref, got_ref, diag_out, lower_out, scale, diag, lower, sems):
    count, width = self_ref.shape[:2]
    scale[pl.ds(0, 1), :] = got_ref[pl.ds(width, 1), :].astype(F32)
    scale[pl.ds(8, count), :] = scale_ref[...].astype(F32)

    def copies(g):
        some = pl.ds(g * group, group)
        return (
            pltpu.make_async_copy(diag.at[some], diag_out.at[some], sems.at[0, g]),
            pltpu.make_async_copy(lower.at[some], lower_out.at[some], sems.at[1, g]),
        )

    first = prev_ref[0] * scale[pl.ds(0, 1), :].astype(BF16)
    lower[0] = lax.dot_general(first, got_ref[pl.ds(0, width), :], NT, preferred_element_type=F32).astype(BF16)

    def turn(g, carry):
        for i in range(group):
            k = g * group + i
            mine, prev, after = self_ref[k], prev_ref[k], prev_ref[jnp.minimum(k + 1, count - 1)]
            here = scale[pl.ds(k + 8, 1), :].astype(BF16)
            back = scale[pl.ds(jnp.where(g == 0, 0, k + 7) if i == 0 else k + 7, 1), :].astype(BF16)
            left = jnp.concatenate(
                [
                    jnp.concatenate([mine * here, prev * back], axis=1),
                    jnp.concatenate([after * here, jnp.zeros_like(after)], axis=1),
                ],
                axis=0,
            )
            both = lax.dot_general(left, jnp.concatenate([mine, prev], axis=1), NT, preferred_element_type=F32)
            diag[k] = both[:width].astype(BF16)
            lower[k + 1] = both[width:].astype(BF16)
        for copy in copies(g):
            copy.start()
        return carry

    lax.fori_loop(0, count // group, turn, 0)

    def finish(g, carry):
        for copy in copies(g):
            copy.wait()
        return carry

    lax.fori_loop(0, count // group, finish, 0)


def cover(cover_self, cover_prev, scaling, got):
    count, width = cover_self.shape[:2]
    group = 16
    hbm, vmem = pl.BlockSpec(memory_space=pltpu.HBM), pl.BlockSpec(memory_space=pltpu.VMEM)
    return pl.pallas_call(
        functools.partial(cover_kernel, group),
        out_shape=[jax.ShapeDtypeStruct(cover_self.shape, BF16)] * 2,
        in_specs=[vmem] * 4,
        out_specs=[hbm, hbm],
        scratch_shapes=[
            pltpu.VMEM((8 + count, width), F32),
            pltpu.VMEM(cover_self.shape, BF16),
            pltpu.VMEM((count + 1, width, width), BF16),
            pltpu.SemaphoreType.DMA((2, count // group)),
        ],
        compiler_params=pltpu.CompilerParams(vmem_limit_bytes=16 * 2**20),
        cost_estimate=pl.CostEstimate(
            flops=2 * count * width * 4 * width * width, bytes_accessed=4 * 2 * count * width * width, transcendentals=0
        ),
        name="cover",
    )(cover_self, cover_prev, scaling, got)


def body(capacity_blocks, capacity_rows, cover_self, cover_prev, scaling):
    n_var, n_own, n_sub = (lax.axis_size(a) for a in AXES)
    got = shifted(jnp.concatenate([cover_self[-1], scaling[-1:]], axis=0), AXES, 1)
    side = CAP * capacity_blocks.shape[2]
    ((keep, send),) = capacity(capacity_blocks, capacity_rows, scaling, ((0, side, "own"),))
    total = keep + swap(send, "sub", 1).astype(F32)
    for axis in ("own", "var"):
        arrived = [swap(total[m].astype(BF16), axis, m) for m in send_order(axis)]
        total = functools.reduce(lambda a, b: a + b.astype(F32), arrived, total[0])
    diag, lower = cover(cover_self, cover_prev, scaling, got)
    return (diag, lower, total)


def solution(mesh):
    split = P(AXES)
    return jax.shard_map(
        body, mesh=mesh, in_specs=(split,) * 5, out_specs=(split,) * 3, check_vma=False
    )
```

```python
import functools

import jax
import jax.numpy as jnp
from jax import lax
from jax.experimental import pallas as pl
from jax.experimental.pallas import tpu as pltpu
from jax.sharding import PartitionSpec as P

CAP = 8
AXES = ("var", "own", "sub")
NT = (((1,), (1,)), ((), ()))
F32, BF16 = jnp.float32, jnp.bfloat16


def swap(value, axis, mask):
    count = lax.axis_size(axis)
    return lax.ppermute(value, axis, [(i, i ^ mask) for i in range(count)])


def shifted(value, axis, steps):
    count = lax.axis_size(axis)
    return lax.ppermute(value, axis, [(i, i + steps) for i in range(count - steps)])


def send_order(axis):
    masks = list(range(1, lax.axis_size(axis)))
    return masks[1:] + masks[:1] if axis == "var" else masks[::-1]


def set_bits(mask, count):
    found = []
    for _ in range(count):
        low = mask & (-mask)
        found.append(31 - lax.clz(low))
        mask = mask ^ low
    return found


def capacity_kernel(step, parts, sizes, rows_ref, cap_ref, scale_ref, *rest):
    outs, (dense, scale_in, scale, acc, sems, scale_sem) = rest[: 2 * len(parts)], rest[2 * len(parts) :]
    count, width = cap_ref.shape[0], cap_ref.shape[2]
    nz = cap_ref.shape[1] // width
    turns = count // step
    side = acc.shape[0]
    tile = 2 * width

    def spot(r):
        return pl.ds(pl.multiple_of(r * width, width), width)

    def lay(k, carry):
        mask = jnp.int32(0)
        for p in range(nz):
            r = rows_ref[p, k]
            mask = mask | jnp.left_shift(jnp.int32(1), r)
            pltpu.make_async_copy(
                cap_ref.at[k, pl.ds(p * width, width), :], dense.at[k, spot(r), :], sems.at[k // step]
            ).start()
        for r in set_bits((1 << CAP) - 1 - mask, CAP - nz):
            dense[k, spot(r), :] = jnp.zeros((width, width), BF16)
        return carry

    fetch = pltpu.make_async_copy(scale_ref, scale_in, scale_sem)
    fetch.start()
    lax.fori_loop(0, count, lay, 0, unroll=4)
    fetch.wait()
    scale[...] = scale_in[...].astype(F32)
    acc[...] = jnp.zeros_like(acc)

    def turn(t, carry):
        first = t * step
        pltpu.make_async_copy(
            cap_ref.at[pl.ds(first, step)],
            dense.at[pl.ds(first, step), pl.ds(0, nz * width), :],
            sems.at[t],
        ).wait()
        ks = [first + i for i in range(step)]
        for j in range(side // tile):
            right = jnp.concatenate(
                [dense[k, pl.ds(tile * j, tile), :] * scale[pl.ds(k, 1), :].astype(BF16) for k in ks], axis=1
            )
            left = jnp.concatenate([dense[k, pl.ds(0, tile * (j + 1)), :] for k in ks], axis=1)
            acc[pl.ds(0, tile * (j + 1)), pl.ds(tile * j, tile)] += lax.dot_general(
                left, right, NT, preferred_element_type=F32
            )
        return carry

    lax.fori_loop(0, turns, turn, 0)
    for i in range(side // tile):
        for j in range(i):
            acc[pl.ds(tile * i, tile), pl.ds(tile * j, tile)] = acc[pl.ds(tile * j, tile), pl.ds(tile * i, tile)].T
    var, own, sub = (lax.axis_index(a) for a in AXES)
    n_var, n_own, held = sizes
    for at, (low, high, first) in enumerate(parts):
        keep_ref, send_ref = outs[2 * at], outs[2 * at + 1]
        for m in range(n_own):

            def emit(v, carry, m=m):
                chip = (var ^ v) * n_own + (own ^ m)
                mine = pl.ds(pl.multiple_of((2 * chip + sub) * held, held), held)
                other = pl.ds(pl.multiple_of((2 * chip + 1 - sub) * held, held), held)
                slot = (m, v) if first == "own" else (v, m)
                keep_ref[slot] = acc[mine, pl.ds(low, high - low)]
                send_ref[slot] = acc[other, pl.ds(low, high - low)].astype(send_ref.dtype)
                return carry

            lax.fori_loop(0, n_var, emit, 0, unroll=True)


def capacity(capacity_blocks, capacity_rows, scaling, parts):
    count, nz, width = capacity_blocks.shape[:3]
    n_var, n_own, n_sub = (lax.axis_size(a) for a in AXES)
    side = CAP * width
    held = side // (n_var * n_own * n_sub)
    step = 32
    sent = BF16 if held % 16 == 0 else F32
    shapes = []
    for low, high, first in parts:
        lead = (n_own, n_var) if first == "own" else (n_var, n_own)
        shapes += [jax.ShapeDtypeStruct(lead + (held, high - low), t) for t in (F32, sent)]
    hbm = pl.BlockSpec(memory_space=pltpu.HBM)
    smem, vmem = pl.BlockSpec(memory_space=pltpu.SMEM), pl.BlockSpec(memory_space=pltpu.VMEM)
    operands = (capacity_rows.T, capacity_blocks.reshape(count, nz * width, width), scaling)
    flops = 2 * side * side * count * width * 5 // 8
    outs = pl.pallas_call(
        functools.partial(capacity_kernel, step, parts, (n_var, n_own, held)),
        out_shape=shapes,
        in_specs=[smem, hbm, hbm],
        out_specs=[vmem] * len(shapes),
        scratch_shapes=[
            pltpu.VMEM((count, side, width), BF16),
            pltpu.VMEM((count, width), BF16),
            pltpu.VMEM((count, width), F32),
            pltpu.VMEM((side, side), F32),
            pltpu.SemaphoreType.DMA((count // step,)),
            pltpu.SemaphoreType.DMA,
        ],
        compiler_params=pltpu.CompilerParams(vmem_limit_bytes=32 * 2**20),
        cost_estimate=pl.CostEstimate(flops=flops, bytes_accessed=14 * 2**20, transcendentals=0),
        name="capacity",
    )(*(pltpu.with_memory_space_constraint(x, pltpu.HBM) for x in operands))
    return [(keep, send.astype(BF16)) for keep, send in zip(outs[0::2], outs[1::2])]


def cover_kernel(group, self_ref, prev_ref, scale_ref, diag_out, lower_out, scale, diag, lower, sems):
    count, width = self_ref.shape[:2]
    scale[pl.ds(0, 8), :] = jnp.zeros((8, width), F32)
    scale[pl.ds(8, count), :] = scale_ref[...].astype(F32)
    lower[0] = jnp.zeros((width, width), BF16)

    def copies(g):
        some = pl.ds(g * group, group)
        return (
            pltpu.make_async_copy(diag.at[some], diag_out.at[some], sems.at[0, g]),
            pltpu.make_async_copy(lower.at[some], lower_out.at[some], sems.at[1, g]),
        )

    def turn(g, carry):
        for i in range(group):
            k = g * group + i
            mine, prev, after = self_ref[k], prev_ref[k], prev_ref[jnp.minimum(k + 1, count - 1)]
            here = scale[pl.ds(k + 8, 1), :].astype(BF16)
            back = scale[pl.ds(k + 7, 1), :].astype(BF16)
            left = jnp.concatenate(
                [
                    jnp.concatenate([mine * here, prev * back], axis=1),
                    jnp.concatenate([after * here, jnp.zeros_like(after)], axis=1),
                ],
                axis=0,
            )
            both = lax.dot_general(left, jnp.concatenate([mine, prev], axis=1), NT, preferred_element_type=F32)
            diag[k] = both[:width].astype(BF16)
            lower[k + 1] = both[width:].astype(BF16)
        for copy in copies(g):
            copy.start()
        return carry

    lax.fori_loop(0, count // group, turn, 0)

    def finish(g, carry):
        for copy in copies(g):
            copy.wait()
        return carry

    lax.fori_loop(0, count // group, finish, 0)


def first_kernel(self_ref, prev_ref, scale_ref, got_ref, diag_in, lower_in, diag_out, lower_out, mine, prev, scale, diag, lower, sems):
    width = mine.shape[1]
    held = [
        pltpu.make_async_copy(self_ref.at[pl.ds(0, 1)], mine, sems.at[0]),
        pltpu.make_async_copy(prev_ref.at[pl.ds(0, 1)], prev, sems.at[1]),
        pltpu.make_async_copy(scale_ref.at[pl.ds(0, 16)], scale, sems.at[2]),
    ]
    for copy in held:
        copy.start()
    for copy in held:
        copy.wait()
    here = scale[...].astype(F32)[0:1].astype(BF16)
    back = got_ref[pl.ds(width, 1), :]
    scaled = prev[0] * back
    left = jnp.concatenate([mine[0] * here, scaled], axis=1)
    right = jnp.concatenate([mine[0], prev[0]], axis=1)
    diag[0] = lax.dot_general(left, right, NT, preferred_element_type=F32).astype(BF16)
    lower[0] = lax.dot_general(scaled, got_ref[pl.ds(0, width), :], NT, preferred_element_type=F32).astype(BF16)
    done = [
        pltpu.make_async_copy(diag, diag_out.at[pl.ds(0, 1)], sems.at[3]),
        pltpu.make_async_copy(lower, lower_out.at[pl.ds(0, 1)], sems.at[4]),
    ]
    for copy in done:
        copy.start()
    for copy in done:
        copy.wait()


def cover(cover_self, cover_prev, scaling):
    count, width = cover_self.shape[:2]
    group = 16
    hbm, vmem = pl.BlockSpec(memory_space=pltpu.HBM), pl.BlockSpec(memory_space=pltpu.VMEM)
    return pl.pallas_call(
        functools.partial(cover_kernel, group),
        out_shape=[jax.ShapeDtypeStruct(cover_self.shape, BF16)] * 2,
        in_specs=[vmem] * 3,
        out_specs=[hbm, hbm],
        scratch_shapes=[
            pltpu.VMEM((8 + count, width), F32),
            pltpu.VMEM(cover_self.shape, BF16),
            pltpu.VMEM((count + 1, width, width), BF16),
            pltpu.SemaphoreType.DMA((2, count // group)),
        ],
        compiler_params=pltpu.CompilerParams(vmem_limit_bytes=16 * 2**20),
        cost_estimate=pl.CostEstimate(
            flops=2 * count * width * 4 * width * width, bytes_accessed=4 * 2 * count * width * width, transcendentals=0
        ),
        name="cover",
    )(cover_self, cover_prev, scaling)


def first_cover(cover_self, cover_prev, scaling, got, diag, lower):
    width = cover_self.shape[1]
    hbm, vmem = pl.BlockSpec(memory_space=pltpu.HBM), pl.BlockSpec(memory_space=pltpu.VMEM)
    block = pltpu.VMEM((1, width, width), BF16)
    cover_self, cover_prev, scaling = (pltpu.with_memory_space_constraint(x, pltpu.HBM) for x in (cover_self, cover_prev, scaling))
    return pl.pallas_call(
        first_kernel,
        out_shape=[jax.ShapeDtypeStruct(x.shape, x.dtype) for x in (diag, lower)],
        in_specs=[hbm, hbm, hbm, vmem, hbm, hbm],
        out_specs=[hbm, hbm],
        input_output_aliases={4: 0, 5: 1},
        scratch_shapes=[block, block, pltpu.VMEM((16, width), BF16), block, block, pltpu.SemaphoreType.DMA((5,))],
        name="first_cover",
    )(cover_self, cover_prev, scaling, got, diag, lower)


def body(capacity_blocks, capacity_rows, cover_self, cover_prev, scaling):
    n_var, n_own, n_sub = (lax.axis_size(a) for a in AXES)
    got = shifted(jnp.concatenate([cover_self[-1], scaling[-1:]], axis=0), AXES, 1)
    side = CAP * capacity_blocks.shape[2]
    ((keep, send),) = capacity(capacity_blocks, capacity_rows, scaling, ((0, side, "own"),))
    total = keep + swap(send, "sub", 1).astype(F32)
    for axis in ("own", "var"):
        arrived = [swap(total[m].astype(BF16), axis, m) for m in send_order(axis)]
        total = functools.reduce(lambda a, b: a + b.astype(F32), arrived, total[0])
        if axis == "own":
            diag, lower = cover(cover_self, cover_prev, scaling)
            total, diag, lower, got = lax.optimization_barrier((total, diag, lower, got))
    diag, lower = first_cover(cover_self, cover_prev, scaling, got, diag, lower)
    return (diag, lower, total)


def solution(mesh):
    split = P(AXES)
    return jax.shard_map(
        body, mesh=mesh, in_specs=(split,) * 5, out_specs=(split,) * 3, check_vma=False
    )
```

```python
import functools

import jax
import jax.numpy as jnp
from jax import lax
from jax.experimental import pallas as pl
from jax.experimental.pallas import tpu as pltpu
from jax.sharding import PartitionSpec as P

CAP = 8
AXES = ("var", "own", "sub")
NT = (((1,), (1,)), ((), ()))
F32, BF16 = jnp.float32, jnp.bfloat16


def swap(value, axis, mask):
    count = lax.axis_size(axis)
    return lax.ppermute(value, axis, [(i, i ^ mask) for i in range(count)])


def shifted(value, axis, steps):
    count = lax.axis_size(axis)
    return lax.ppermute(value, axis, [(i, i + steps) for i in range(count - steps)])


def send_order(axis):
    masks = list(range(1, lax.axis_size(axis)))
    return masks[1:] + masks[:1] if axis == "var" else masks[::-1]


def set_bits(mask, count):
    found = []
    for _ in range(count):
        low = mask & (-mask)
        found.append(31 - lax.clz(low))
        mask = mask ^ low
    return found


def multiply(dense, scale, acc, ks, low, tile):
    side = dense.shape[1]
    for j in range(low, low + acc.shape[1] // tile):
        right = jnp.concatenate(
            [dense[k, pl.ds(tile * j, tile), :] * scale[pl.ds(k, 1), :].astype(BF16) for k in ks], axis=1
        )
        under = pl.ds(tile * j, side - tile * j)
        left = jnp.concatenate([dense[k, under, :] for k in ks], axis=1)
        acc[under, pl.ds(tile * (j - low), tile)] += lax.dot_general(left, right, NT, preferred_element_type=F32)


def emit(acc, keep_ref, send_ref, order):
    var, own, sub = (lax.axis_index(a) for a in AXES)
    n_var, n_own = (keep_ref.shape[1], keep_ref.shape[0]) if order == "own" else keep_ref.shape[:2]
    held = keep_ref.shape[2]
    for m in range(n_own):

        def one(v, carry, m=m):
            chip = (var ^ v) * n_own + (own ^ m)
            slot = (m, v) if order == "own" else (v, m)
            keep_ref[slot] = acc[pl.ds(pl.multiple_of((2 * chip + sub) * held, held), held), :]
            send_ref[slot] = acc[pl.ds(pl.multiple_of((2 * chip + 1 - sub) * held, held), held), :].astype(send_ref.dtype)
            return carry

        lax.fori_loop(0, n_var, one, 0, unroll=True)


def left_kernel(step, order, rows_ref, cap_ref, scale_ref, dense, scale, acc, keep_ref, send_ref, scale_in, sems, scale_sem):
    count, width = cap_ref.shape[0], cap_ref.shape[2]
    nz = cap_ref.shape[1] // width
    tile = 2 * width

    def spot(r):
        return pl.ds(pl.multiple_of(r * width, width), width)

    def lay(k, carry):
        mask = jnp.int32(0)
        for p in range(nz):
            r = rows_ref[p, k]
            mask = mask | jnp.left_shift(jnp.int32(1), r)
            pltpu.make_async_copy(
                cap_ref.at[k, pl.ds(p * width, width), :], dense.at[k, spot(r), :], sems.at[k // step]
            ).start()
        for r in set_bits((1 << CAP) - 1 - mask, CAP - nz):
            dense[k, spot(r), :] = jnp.zeros((width, width), BF16)
        return carry

    fetch = pltpu.make_async_copy(scale_ref, scale_in, scale_sem)
    fetch.start()
    lax.fori_loop(0, count, lay, 0, unroll=4)
    fetch.wait()
    scale[...] = scale_in[...].astype(F32)
    acc[...] = jnp.zeros_like(acc)

    def turn(t, carry):
        first = t * step
        pltpu.make_async_copy(
            cap_ref.at[pl.ds(first, step)],
            dense.at[pl.ds(first, step), pl.ds(0, nz * width), :],
            sems.at[t],
        ).wait()
        multiply(dense, scale, acc, [first + i for i in range(step)], 0, tile)
        return carry

    lax.fori_loop(0, count // step, turn, 0)
    for j in range(acc.shape[1] // tile):
        for i in range(j):
            acc[pl.ds(tile * i, tile), pl.ds(tile * j, tile)] = acc[pl.ds(tile * j, tile), pl.ds(tile * i, tile)].T
    emit(acc, keep_ref, send_ref, order)


def right_kernel(step, order, dense, scale, before, keep_ref, send_ref, acc):
    count, tile = dense.shape[0], 2 * dense.shape[2]
    low = before.shape[1] // tile
    acc[...] = jnp.zeros_like(acc)

    def turn(t, carry):
        multiply(dense, scale, acc, [t * step + i for i in range(step)], low, tile)
        return carry

    lax.fori_loop(0, count // step, turn, 0)
    for j in range(low, low + acc.shape[1] // tile):
        for i in range(j):
            source, at = (before, i) if i < low else (acc, i - low)
            acc[pl.ds(tile * i, tile), pl.ds(tile * (j - low), tile)] = source[pl.ds(tile * j, tile), pl.ds(tile * at, tile)].T
    emit(acc, keep_ref, send_ref, order)


def capacity(capacity_blocks, capacity_rows, scaling, cut, orders):
    count, nz, width = capacity_blocks.shape[:3]
    n_var, n_own, n_sub = (lax.axis_size(a) for a in AXES)
    side = CAP * width
    held = side // (n_var * n_own * n_sub)
    step = 32
    sent = BF16 if held % 16 == 0 else F32

    def shapes(columns, order):
        lead = (n_own, n_var) if order == "own" else (n_var, n_own)
        return [jax.ShapeDtypeStruct(lead + (held, columns), t) for t in (F32, sent)]

    hbm = pl.BlockSpec(memory_space=pltpu.HBM)
    smem, vmem = pl.BlockSpec(memory_space=pltpu.SMEM), pl.BlockSpec(memory_space=pltpu.VMEM)
    operands = (capacity_rows.T, capacity_blocks.reshape(count, nz * width, width), scaling)
    dense, scale, left, *first = pl.pallas_call(
        functools.partial(left_kernel, step, orders[0]),
        out_shape=[
            pltpu.VMEM((count, side, width), BF16),
            pltpu.VMEM((count, width), F32),
            pltpu.VMEM((side, cut), F32),
            *shapes(cut, orders[0]),
        ],
        in_specs=[smem, hbm, hbm],
        out_specs=[vmem] * 5,
        scratch_shapes=[
            pltpu.VMEM((count, width), BF16),
            pltpu.SemaphoreType.DMA((count // step,)),
            pltpu.SemaphoreType.DMA,
        ],
        compiler_params=pltpu.CompilerParams(vmem_limit_bytes=30 * 2**20),
        cost_estimate=pl.CostEstimate(flops=2 * side * cut * count * width, bytes_accessed=14 * 2**20, transcendentals=0),
        name="capacity_left",
    )(*(pltpu.with_memory_space_constraint(x, pltpu.HBM) for x in operands))
    second = pl.pallas_call(
        functools.partial(right_kernel, step, orders[1]),
        out_shape=shapes(side - cut, orders[1]),
        in_specs=[vmem] * 3,
        out_specs=[vmem] * 2,
        scratch_shapes=[pltpu.VMEM((side, side - cut), F32)],
        compiler_params=pltpu.CompilerParams(vmem_limit_bytes=30 * 2**20),
        cost_estimate=pl.CostEstimate(flops=2 * side * cut * count * width, bytes_accessed=2**20, transcendentals=0),
        name="capacity_right",
    )(*(pltpu.with_memory_space_constraint(x, pltpu.VMEM) for x in (dense, scale, left)))
    return [(keep, send.astype(BF16)) for keep, send in (first, second)]


def cover_kernel(group, self_ref, prev_ref, scale_ref, diag_out, lower_out, scale, diag, lower, sems):
    count, width = self_ref.shape[:2]
    scale[pl.ds(0, 8), :] = jnp.zeros((8, width), F32)
    scale[pl.ds(8, count), :] = scale_ref[...].astype(F32)
    lower[0] = jnp.zeros((width, width), BF16)

    def copies(g):
        some = pl.ds(g * group, group)
        return (
            pltpu.make_async_copy(diag.at[some], diag_out.at[some], sems.at[0, g]),
            pltpu.make_async_copy(lower.at[some], lower_out.at[some], sems.at[1, g]),
        )

    def turn(g, carry):
        for i in range(group):
            k = g * group + i
            mine, prev, after = self_ref[k], prev_ref[k], prev_ref[jnp.minimum(k + 1, count - 1)]
            here = scale[pl.ds(k + 8, 1), :].astype(BF16)
            back = scale[pl.ds(k + 7, 1), :].astype(BF16)
            left = jnp.concatenate(
                [
                    jnp.concatenate([mine * here, prev * back], axis=1),
                    jnp.concatenate([after * here, jnp.zeros_like(after)], axis=1),
                ],
                axis=0,
            )
            both = lax.dot_general(left, jnp.concatenate([mine, prev], axis=1), NT, preferred_element_type=F32)
            diag[k] = both[:width].astype(BF16)
            lower[k + 1] = both[width:].astype(BF16)
        for copy in copies(g):
            copy.start()
        return carry

    lax.fori_loop(0, count // group, turn, 0)

    def finish(g, carry):
        for copy in copies(g):
            copy.wait()
        return carry

    lax.fori_loop(0, count // group, finish, 0)


def first_kernel(self_ref, prev_ref, scale_ref, got_ref, diag_in, lower_in, diag_out, lower_out, mine, prev, scale, diag, lower, sems):
    width = mine.shape[1]
    held = [
        pltpu.make_async_copy(self_ref.at[pl.ds(0, 1)], mine, sems.at[0]),
        pltpu.make_async_copy(prev_ref.at[pl.ds(0, 1)], prev, sems.at[1]),
        pltpu.make_async_copy(scale_ref.at[pl.ds(0, 16)], scale, sems.at[2]),
    ]
    for copy in held:
        copy.start()
    for copy in held:
        copy.wait()
    here = scale[...].astype(F32)[0:1].astype(BF16)
    back = got_ref[pl.ds(width, 1), :]
    scaled = prev[0] * back
    left = jnp.concatenate([mine[0] * here, scaled], axis=1)
    right = jnp.concatenate([mine[0], prev[0]], axis=1)
    diag[0] = lax.dot_general(left, right, NT, preferred_element_type=F32).astype(BF16)
    lower[0] = lax.dot_general(scaled, got_ref[pl.ds(0, width), :], NT, preferred_element_type=F32).astype(BF16)
    done = [
        pltpu.make_async_copy(diag, diag_out.at[pl.ds(0, 1)], sems.at[3]),
        pltpu.make_async_copy(lower, lower_out.at[pl.ds(0, 1)], sems.at[4]),
    ]
    for copy in done:
        copy.start()
    for copy in done:
        copy.wait()


def cover(cover_self, cover_prev, scaling):
    count, width = cover_self.shape[:2]
    group = 16
    hbm, vmem = pl.BlockSpec(memory_space=pltpu.HBM), pl.BlockSpec(memory_space=pltpu.VMEM)
    return pl.pallas_call(
        functools.partial(cover_kernel, group),
        out_shape=[jax.ShapeDtypeStruct(cover_self.shape, BF16)] * 2,
        in_specs=[vmem] * 3,
        out_specs=[hbm, hbm],
        scratch_shapes=[
            pltpu.VMEM((8 + count, width), F32),
            pltpu.VMEM(cover_self.shape, BF16),
            pltpu.VMEM((count + 1, width, width), BF16),
            pltpu.SemaphoreType.DMA((2, count // group)),
        ],
        compiler_params=pltpu.CompilerParams(vmem_limit_bytes=16 * 2**20),
        cost_estimate=pl.CostEstimate(
            flops=2 * count * width * 4 * width * width, bytes_accessed=4 * 2 * count * width * width, transcendentals=0
        ),
        name="cover",
    )(cover_self, cover_prev, scaling)


def first_cover(cover_self, cover_prev, scaling, got, diag, lower):
    width = cover_self.shape[1]
    hbm, vmem = pl.BlockSpec(memory_space=pltpu.HBM), pl.BlockSpec(memory_space=pltpu.VMEM)
    block = pltpu.VMEM((1, width, width), BF16)
    cover_self, cover_prev, scaling = (pltpu.with_memory_space_constraint(x, pltpu.HBM) for x in (cover_self, cover_prev, scaling))
    return pl.pallas_call(
        first_kernel,
        out_shape=[jax.ShapeDtypeStruct(x.shape, x.dtype) for x in (diag, lower)],
        in_specs=[hbm, hbm, hbm, vmem, hbm, hbm],
        out_specs=[hbm, hbm],
        input_output_aliases={4: 0, 5: 1},
        scratch_shapes=[block, block, pltpu.VMEM((16, width), BF16), block, block, pltpu.SemaphoreType.DMA((5,))],
        name="first_cover",
    )(cover_self, cover_prev, scaling, got, diag, lower)


def body(capacity_blocks, capacity_rows, cover_self, cover_prev, scaling):
    n_var, n_own, n_sub = (lax.axis_size(a) for a in AXES)
    tail = jnp.concatenate([cover_self[-1], scaling[-1:]], axis=0)
    side = CAP * capacity_blocks.shape[2]
    sums = capacity(capacity_blocks, capacity_rows, scaling, side // 4 * 3, ("own", "own"))
    received = [swap(send, "sub", 1) for _, send in sums]
    received, tail, covered = lax.optimization_barrier((received, tail, (cover_self, cover_prev, scaling)))
    total = jnp.concatenate([keep + term.astype(F32) for (keep, _), term in zip(sums, received)], axis=-1)
    got = shifted(tail, AXES, 1)
    for axis in ("own", "var"):
        arrived = [swap(total[m].astype(BF16), axis, m) for m in send_order(axis)]
        total = functools.reduce(lambda a, b: a + b.astype(F32), arrived, total[0])
        if axis == "own":
            diag, lower = cover(*covered)
            total, diag, lower, got = lax.optimization_barrier((total, diag, lower, got))
    diag, lower = first_cover(cover_self, cover_prev, scaling, got, diag, lower)
    return (diag, lower, total)


def solution(mesh):
    split = P(AXES)
    return jax.shard_map(
        body, mesh=mesh, in_specs=(split,) * 5, out_specs=(split,) * 3, check_vma=False
    )
```

```python
import functools

import jax
import jax.numpy as jnp
from jax import lax
from jax.experimental import pallas as pl
from jax.experimental.pallas import tpu as pltpu
from jax.sharding import PartitionSpec as P

CAP = 8
AXES = ("var", "own", "sub")
NT = (((1,), (1,)), ((), ()))
F32, BF16 = jnp.float32, jnp.bfloat16


def swap(value, axis, mask):
    count = lax.axis_size(axis)
    return lax.ppermute(value, axis, [(i, i ^ mask) for i in range(count)])


def shifted(value, axis, steps):
    count = lax.axis_size(axis)
    return lax.ppermute(value, axis, [(i, i + steps) for i in range(count - steps)])


def send_order(axis):
    masks = list(range(1, lax.axis_size(axis)))
    return masks[1:] + masks[:1] if axis == "var" else masks[::-1]


def set_bits(mask, count):
    found = []
    for _ in range(count):
        low = mask & (-mask)
        found.append(31 - lax.clz(low))
        mask = mask ^ low
    return found


def multiply(dense, scale, acc, ks, low, tile):
    side = dense.shape[1]
    for j in range(low, low + acc.shape[1] // tile):
        right = jnp.concatenate(
            [dense[k, pl.ds(tile * j, tile), :] * scale[pl.ds(k, 1), :].astype(BF16) for k in ks], axis=1
        )
        under = pl.ds(tile * j, side - tile * j)
        left = jnp.concatenate([dense[k, under, :] for k in ks], axis=1)
        acc[under, pl.ds(tile * (j - low), tile)] += lax.dot_general(left, right, NT, preferred_element_type=F32)


def emit(acc, keep_ref, send_ref, order):
    var, own, sub = (lax.axis_index(a) for a in AXES)
    n_var, n_own = (keep_ref.shape[1], keep_ref.shape[0]) if order == "own" else keep_ref.shape[:2]
    held = keep_ref.shape[2]
    for m in range(n_own):

        def one(v, carry, m=m):
            chip = (var ^ v) * n_own + (own ^ m)
            slot = (m, v) if order == "own" else (v, m)
            keep_ref[slot] = acc[pl.ds(pl.multiple_of((2 * chip + sub) * held, held), held), :].astype(keep_ref.dtype)
            send_ref[slot] = acc[pl.ds(pl.multiple_of((2 * chip + 1 - sub) * held, held), held), :].astype(send_ref.dtype)
            return carry

        lax.fori_loop(0, n_var, one, 0, unroll=True)


def left_kernel(step, order, rows_ref, cap_ref, scale_ref, dense, scale, acc, keep_ref, send_ref, scale_in, sems, scale_sem):
    count, width = cap_ref.shape[0], cap_ref.shape[2]
    nz = cap_ref.shape[1] // width
    tile = 2 * width

    def spot(r):
        return pl.ds(pl.multiple_of(r * width, width), width)

    def lay(k, carry):
        mask = jnp.int32(0)
        for p in range(nz):
            r = rows_ref[p, k]
            mask = mask | jnp.left_shift(jnp.int32(1), r)
            pltpu.make_async_copy(
                cap_ref.at[k, pl.ds(p * width, width), :], dense.at[k, spot(r), :], sems.at[k // step]
            ).start()
        for r in set_bits((1 << CAP) - 1 - mask, CAP - nz):
            dense[k, spot(r), :] = jnp.zeros((width, width), BF16)
        return carry

    fetch = pltpu.make_async_copy(scale_ref, scale_in, scale_sem)
    fetch.start()
    lax.fori_loop(0, count, lay, 0, unroll=4)
    fetch.wait()
    scale[...] = scale_in[...].astype(F32)
    acc[...] = jnp.zeros_like(acc)

    def turn(t, carry):
        first = t * step
        pltpu.make_async_copy(
            cap_ref.at[pl.ds(first, step)],
            dense.at[pl.ds(first, step), pl.ds(0, nz * width), :],
            sems.at[t],
        ).wait()
        multiply(dense, scale, acc, [first + i for i in range(step)], 0, tile)
        return carry

    lax.fori_loop(0, count // step, turn, 0)
    for j in range(acc.shape[1] // tile):
        for i in range(j):
            acc[pl.ds(tile * i, tile), pl.ds(tile * j, tile)] = acc[pl.ds(tile * j, tile), pl.ds(tile * i, tile)].T
    emit(acc, keep_ref, send_ref, order)


def right_kernel(step, order, dense, scale, before, keep_ref, send_ref, acc):
    count, tile = dense.shape[0], 2 * dense.shape[2]
    low = before.shape[1] // tile
    acc[...] = jnp.zeros_like(acc)

    def turn(t, carry):
        multiply(dense, scale, acc, [t * step + i for i in range(step)], low, tile)
        return carry

    lax.fori_loop(0, count // step, turn, 0)
    for j in range(low, low + acc.shape[1] // tile):
        for i in range(j):
            source, at = (before, i) if i < low else (acc, i - low)
            acc[pl.ds(tile * i, tile), pl.ds(tile * (j - low), tile)] = source[pl.ds(tile * j, tile), pl.ds(tile * at, tile)].T
    emit(acc, keep_ref, send_ref, order)


def capacity(capacity_blocks, capacity_rows, scaling, cut, orders):
    count, nz, width = capacity_blocks.shape[:3]
    n_var, n_own, n_sub = (lax.axis_size(a) for a in AXES)
    side = CAP * width
    held = side // (n_var * n_own * n_sub)
    step = 32
    sent = BF16 if held % 16 == 0 else F32

    def shapes(columns, order):
        lead = (n_own, n_var) if order == "own" else (n_var, n_own)
        return [jax.ShapeDtypeStruct(lead + (held, columns), t) for t in (sent, sent)]

    hbm = pl.BlockSpec(memory_space=pltpu.HBM)
    smem, vmem = pl.BlockSpec(memory_space=pltpu.SMEM), pl.BlockSpec(memory_space=pltpu.VMEM)
    operands = (capacity_rows.T, capacity_blocks.reshape(count, nz * width, width), scaling)
    dense, scale, left, *first = pl.pallas_call(
        functools.partial(left_kernel, step, orders[0]),
        out_shape=[
            pltpu.VMEM((count, side, width), BF16),
            pltpu.VMEM((count, width), F32),
            pltpu.VMEM((side, cut), F32),
            *shapes(cut, orders[0]),
        ],
        in_specs=[smem, hbm, hbm],
        out_specs=[vmem] * 5,
        scratch_shapes=[
            pltpu.VMEM((count, width), BF16),
            pltpu.SemaphoreType.DMA((count // step,)),
            pltpu.SemaphoreType.DMA,
        ],
        compiler_params=pltpu.CompilerParams(vmem_limit_bytes=30 * 2**20),
        cost_estimate=pl.CostEstimate(flops=2 * side * cut * count * width, bytes_accessed=14 * 2**20, transcendentals=0),
        name="capacity_left",
    )(*(pltpu.with_memory_space_constraint(x, pltpu.HBM) for x in operands))
    second = pl.pallas_call(
        functools.partial(right_kernel, step, orders[1]),
        out_shape=shapes(side - cut, orders[1]),
        in_specs=[vmem] * 3,
        out_specs=[vmem] * 2,
        scratch_shapes=[pltpu.VMEM((side, side - cut), F32)],
        compiler_params=pltpu.CompilerParams(vmem_limit_bytes=30 * 2**20),
        cost_estimate=pl.CostEstimate(flops=2 * side * cut * count * width, bytes_accessed=2**20, transcendentals=0),
        name="capacity_right",
    )(*(pltpu.with_memory_space_constraint(x, pltpu.VMEM) for x in (dense, scale, left)))
    return [(keep, send.astype(BF16)) for keep, send in (first, second)]


def join_kernel(n_parts, *refs):
    kept, received, outs = refs[:n_parts], refs[n_parts : 2 * n_parts], refs[2 * n_parts :]

    def one(v, carry):
        for m in range(kept[0].shape[0]):
            out, low = outs[m], 0
            for keep_ref, got_ref in zip(kept, received):
                high = low + keep_ref.shape[3]
                out[v, :, low:high] = (keep_ref[m, v].astype(F32) + got_ref[m, v].astype(F32)).astype(out.dtype)
                low = high
        return carry

    lax.fori_loop(0, kept[0].shape[1], one, 0)


def join(kept, received):
    n_own, n_var, held = kept[0].shape[:3]
    side = sum(x.shape[3] for x in kept)
    sent = BF16 if held % 16 == 0 else F32
    vmem = pl.BlockSpec(memory_space=pltpu.VMEM)
    return pl.pallas_call(
        functools.partial(join_kernel, len(kept)),
        out_shape=[jax.ShapeDtypeStruct((n_var, held, side), sent if m else F32) for m in range(n_own)],
        in_specs=[vmem] * (2 * len(kept)),
        out_specs=[vmem] * n_own,
        compiler_params=pltpu.CompilerParams(vmem_limit_bytes=16 * 2**20),
        name="join",
    )(*kept, *received)


def cover_kernel(group, self_ref, prev_ref, scale_ref, diag_out, lower_out, scale, diag, lower, sems):
    count, width = self_ref.shape[:2]
    scale[pl.ds(0, 8), :] = jnp.zeros((8, width), F32)
    scale[pl.ds(8, count), :] = scale_ref[...].astype(F32)
    lower[0] = jnp.zeros((width, width), BF16)

    def copies(g):
        some = pl.ds(g * group, group)
        return (
            pltpu.make_async_copy(diag.at[some], diag_out.at[some], sems.at[0, g]),
            pltpu.make_async_copy(lower.at[some], lower_out.at[some], sems.at[1, g]),
        )

    def turn(g, carry):
        for i in range(group):
            k = g * group + i
            mine, prev, after = self_ref[k], prev_ref[k], prev_ref[jnp.minimum(k + 1, count - 1)]
            here = scale[pl.ds(k + 8, 1), :].astype(BF16)
            back = scale[pl.ds(k + 7, 1), :].astype(BF16)
            left = jnp.concatenate(
                [
                    jnp.concatenate([mine * here, prev * back], axis=1),
                    jnp.concatenate([after * here, jnp.zeros_like(after)], axis=1),
                ],
                axis=0,
            )
            both = lax.dot_general(left, jnp.concatenate([mine, prev], axis=1), NT, preferred_element_type=F32)
            diag[k] = both[:width].astype(BF16)
            lower[k + 1] = both[width:].astype(BF16)
        for copy in copies(g):
            copy.start()
        return carry

    lax.fori_loop(0, count // group, turn, 0)

    def finish(g, carry):
        for copy in copies(g):
            copy.wait()
        return carry

    lax.fori_loop(0, count // group, finish, 0)


def first_kernel(self_ref, prev_ref, scale_ref, got_ref, diag_in, lower_in, diag_out, lower_out, mine, prev, scale, diag, lower, sems):
    width = mine.shape[1]
    held = [
        pltpu.make_async_copy(self_ref.at[pl.ds(0, 1)], mine, sems.at[0]),
        pltpu.make_async_copy(prev_ref.at[pl.ds(0, 1)], prev, sems.at[1]),
        pltpu.make_async_copy(scale_ref.at[pl.ds(0, 16)], scale, sems.at[2]),
    ]
    for copy in held:
        copy.start()
    for copy in held:
        copy.wait()
    here = scale[...].astype(F32)[0:1].astype(BF16)
    back = got_ref[pl.ds(width, 1), :]
    scaled = prev[0] * back
    left = jnp.concatenate([mine[0] * here, scaled], axis=1)
    right = jnp.concatenate([mine[0], prev[0]], axis=1)
    diag[0] = lax.dot_general(left, right, NT, preferred_element_type=F32).astype(BF16)
    lower[0] = lax.dot_general(scaled, got_ref[pl.ds(0, width), :], NT, preferred_element_type=F32).astype(BF16)
    done = [
        pltpu.make_async_copy(diag, diag_out.at[pl.ds(0, 1)], sems.at[3]),
        pltpu.make_async_copy(lower, lower_out.at[pl.ds(0, 1)], sems.at[4]),
    ]
    for copy in done:
        copy.start()
    for copy in done:
        copy.wait()


def cover(cover_self, cover_prev, scaling):
    count, width = cover_self.shape[:2]
    group = 16
    hbm, vmem = pl.BlockSpec(memory_space=pltpu.HBM), pl.BlockSpec(memory_space=pltpu.VMEM)
    return pl.pallas_call(
        functools.partial(cover_kernel, group),
        out_shape=[jax.ShapeDtypeStruct(cover_self.shape, BF16)] * 2,
        in_specs=[vmem] * 3,
        out_specs=[hbm, hbm],
        scratch_shapes=[
            pltpu.VMEM((8 + count, width), F32),
            pltpu.VMEM(cover_self.shape, BF16),
            pltpu.VMEM((count + 1, width, width), BF16),
            pltpu.SemaphoreType.DMA((2, count // group)),
        ],
        compiler_params=pltpu.CompilerParams(vmem_limit_bytes=16 * 2**20),
        cost_estimate=pl.CostEstimate(
            flops=2 * count * width * 4 * width * width, bytes_accessed=4 * 2 * count * width * width, transcendentals=0
        ),
        name="cover",
    )(cover_self, cover_prev, scaling)


def first_cover(cover_self, cover_prev, scaling, got, diag, lower):
    width = cover_self.shape[1]
    hbm, vmem = pl.BlockSpec(memory_space=pltpu.HBM), pl.BlockSpec(memory_space=pltpu.VMEM)
    block = pltpu.VMEM((1, width, width), BF16)
    cover_self, cover_prev, scaling = (pltpu.with_memory_space_constraint(x, pltpu.HBM) for x in (cover_self, cover_prev, scaling))
    return pl.pallas_call(
        first_kernel,
        out_shape=[jax.ShapeDtypeStruct(x.shape, x.dtype) for x in (diag, lower)],
        in_specs=[hbm, hbm, hbm, vmem, hbm, hbm],
        out_specs=[hbm, hbm],
        input_output_aliases={4: 0, 5: 1},
        scratch_shapes=[block, block, pltpu.VMEM((16, width), BF16), block, block, pltpu.SemaphoreType.DMA((5,))],
        name="first_cover",
    )(cover_self, cover_prev, scaling, got, diag, lower)


def body(capacity_blocks, capacity_rows, cover_self, cover_prev, scaling):
    n_var, n_own, n_sub = (lax.axis_size(a) for a in AXES)
    tail = jnp.concatenate([cover_self[-1], scaling[-1:]], axis=0)
    side = CAP * capacity_blocks.shape[2]
    sums = capacity(capacity_blocks, capacity_rows, scaling, side // 4 * 3, ("own", "own"))
    received = [swap(send, "sub", 1) for _, send in sums]
    received, tail, covered = lax.optimization_barrier((received, tail, (cover_self, cover_prev, scaling)))
    total = join([keep for keep, _ in sums], received)
    got = shifted(tail, AXES, 1)
    for axis in ("own", "var"):
        arrived = [swap(total[m].astype(BF16), axis, m) for m in send_order(axis)]
        total = functools.reduce(lambda a, b: a + b.astype(F32), arrived, total[0])
        if axis == "own":
            diag, lower = cover(*covered)
            total, diag, lower, got = lax.optimization_barrier((total, diag, lower, got))
    diag, lower = first_cover(cover_self, cover_prev, scaling, got, diag, lower)
    return (diag, lower, total)


def solution(mesh):
    split = P(AXES)
    return jax.shard_map(
        body, mesh=mesh, in_specs=(split,) * 5, out_specs=(split,) * 3, check_vma=False
    )
```

```python
import functools

import jax
import jax.numpy as jnp
from jax import lax
from jax.experimental import pallas as pl
from jax.experimental.pallas import tpu as pltpu
from jax.sharding import PartitionSpec as P

CAP = 8
AXES = ("var", "own", "sub")
NT = (((1,), (1,)), ((), ()))
F32, BF16 = jnp.float32, jnp.bfloat16


def swap(value, axis, mask):
    count = lax.axis_size(axis)
    return lax.ppermute(value, axis, [(i, i ^ mask) for i in range(count)])


def shifted(value, axis, steps):
    count = lax.axis_size(axis)
    return lax.ppermute(value, axis, [(i, i + steps) for i in range(count - steps)])


def send_order(axis):
    masks = list(range(1, lax.axis_size(axis)))
    return masks[1:] + masks[:1] if axis == "var" else masks[::-1]


def set_bits(mask, count):
    found = []
    for _ in range(count):
        low = mask & (-mask)
        found.append(31 - lax.clz(low))
        mask = mask ^ low
    return found


def multiply(dense, scale, acc, ks, low, tile):
    side = dense.shape[1]
    for j in range(low, low + acc.shape[1] // tile):
        right = jnp.concatenate(
            [dense[k, pl.ds(tile * j, tile), :] * scale[pl.ds(k, 1), :].astype(BF16) for k in ks], axis=1
        )
        under = pl.ds(tile * j, side - tile * j)
        left = jnp.concatenate([dense[k, under, :] for k in ks], axis=1)
        acc[under, pl.ds(tile * (j - low), tile)] += lax.dot_general(left, right, NT, preferred_element_type=F32)


def emit(acc, keep_ref, send_ref, order):
    var, own, sub = (lax.axis_index(a) for a in AXES)
    n_var, n_own = (keep_ref.shape[1], keep_ref.shape[0]) if order == "own" else keep_ref.shape[:2]
    held = keep_ref.shape[2]
    for m in range(n_own):

        def one(v, carry, m=m):
            chip = (var ^ v) * n_own + (own ^ m)
            slot = (m, v) if order == "own" else (v, m)
            keep_ref[slot] = acc[pl.ds(pl.multiple_of((2 * chip + sub) * held, held), held), :].astype(keep_ref.dtype)
            send_ref[slot] = acc[pl.ds(pl.multiple_of((2 * chip + 1 - sub) * held, held), held), :].astype(send_ref.dtype)
            return carry

        lax.fori_loop(0, n_var, one, 0, unroll=True)


def left_kernel(step, order, rows_ref, cap_ref, scale_ref, dense, scale, acc, keep_ref, send_ref, scale_in, sems, scale_sem):
    count, width = cap_ref.shape[0], cap_ref.shape[2]
    nz = cap_ref.shape[1] // width
    tile = 2 * width

    def spot(r):
        return pl.ds(pl.multiple_of(r * width, width), width)

    def lay(k, carry):
        mask = jnp.int32(0)
        for p in range(nz):
            r = rows_ref[p, k]
            mask = mask | jnp.left_shift(jnp.int32(1), r)
            pltpu.make_async_copy(
                cap_ref.at[k, pl.ds(p * width, width), :], dense.at[k, spot(r), :], sems.at[k // step]
            ).start()
        for r in set_bits((1 << CAP) - 1 - mask, CAP - nz):
            dense[k, spot(r), :] = jnp.zeros((width, width), BF16)
        return carry

    fetch = pltpu.make_async_copy(scale_ref, scale_in, scale_sem)
    fetch.start()
    lax.fori_loop(0, count, lay, 0, unroll=4)
    fetch.wait()
    scale[...] = scale_in[...].astype(F32)
    acc[...] = jnp.zeros_like(acc)

    def turn(t, carry):
        first = t * step
        pltpu.make_async_copy(
            cap_ref.at[pl.ds(first, step)],
            dense.at[pl.ds(first, step), pl.ds(0, nz * width), :],
            sems.at[t],
        ).wait()
        multiply(dense, scale, acc, [first + i for i in range(step)], 0, tile)
        return carry

    lax.fori_loop(0, count // step, turn, 0)
    for j in range(acc.shape[1] // tile):
        for i in range(j):
            acc[pl.ds(tile * i, tile), pl.ds(tile * j, tile)] = acc[pl.ds(tile * j, tile), pl.ds(tile * i, tile)].T
    emit(acc, keep_ref, send_ref, order)


def right_kernel(step, order, dense, scale, before, keep_ref, send_ref, acc):
    count, tile = dense.shape[0], 2 * dense.shape[2]
    low = before.shape[1] // tile
    acc[...] = jnp.zeros_like(acc)
    multiply(dense, scale, acc, range(count), low, tile)
    for j in range(low, low + acc.shape[1] // tile):
        for i in range(j):
            source, at = (before, i) if i < low else (acc, i - low)
            acc[pl.ds(tile * i, tile), pl.ds(tile * (j - low), tile)] = source[pl.ds(tile * j, tile), pl.ds(tile * at, tile)].T
    emit(acc, keep_ref, send_ref, order)


def capacity(capacity_blocks, capacity_rows, scaling, cut, orders):
    count, nz, width = capacity_blocks.shape[:3]
    n_var, n_own, n_sub = (lax.axis_size(a) for a in AXES)
    side = CAP * width
    held = side // (n_var * n_own * n_sub)
    step = 32
    sent = BF16 if held % 16 == 0 else F32

    def shapes(columns, order):
        lead = (n_own, n_var) if order == "own" else (n_var, n_own)
        return [jax.ShapeDtypeStruct(lead + (held, columns), t) for t in (sent, sent)]

    hbm = pl.BlockSpec(memory_space=pltpu.HBM)
    smem, vmem = pl.BlockSpec(memory_space=pltpu.SMEM), pl.BlockSpec(memory_space=pltpu.VMEM)
    operands = (capacity_rows.T, capacity_blocks.reshape(count, nz * width, width), scaling)
    dense, scale, left, *first = pl.pallas_call(
        functools.partial(left_kernel, step, orders[0]),
        out_shape=[
            pltpu.VMEM((count, side, width), BF16),
            pltpu.VMEM((count, width), F32),
            pltpu.VMEM((side, cut), F32),
            *shapes(cut, orders[0]),
        ],
        in_specs=[smem, hbm, hbm],
        out_specs=[vmem] * 5,
        scratch_shapes=[
            pltpu.VMEM((count, width), BF16),
            pltpu.SemaphoreType.DMA((count // step,)),
            pltpu.SemaphoreType.DMA,
        ],
        compiler_params=pltpu.CompilerParams(vmem_limit_bytes=30 * 2**20),
        cost_estimate=pl.CostEstimate(flops=2 * side * cut * count * width, bytes_accessed=14 * 2**20, transcendentals=0),
        name="capacity_left",
    )(*(pltpu.with_memory_space_constraint(x, pltpu.HBM) for x in operands))
    second = pl.pallas_call(
        functools.partial(right_kernel, step, orders[1]),
        out_shape=shapes(side - cut, orders[1]),
        in_specs=[vmem] * 3,
        out_specs=[vmem] * 2,
        scratch_shapes=[pltpu.VMEM((side, side - cut), F32)],
        compiler_params=pltpu.CompilerParams(vmem_limit_bytes=30 * 2**20),
        cost_estimate=pl.CostEstimate(flops=2 * side * cut * count * width, bytes_accessed=2**20, transcendentals=0),
        name="capacity_right",
    )(*(pltpu.with_memory_space_constraint(x, pltpu.VMEM) for x in (dense, scale, left)))
    return [(keep, send.astype(BF16)) for keep, send in (first, second)]


def join_kernel(n_parts, *refs):
    kept, received, outs = refs[:n_parts], refs[n_parts : 2 * n_parts], refs[2 * n_parts :]

    def one(v, carry):
        for m in range(kept[0].shape[0]):
            out, low = outs[m], 0
            for keep_ref, got_ref in zip(kept, received):
                high = low + keep_ref.shape[3]
                out[v, :, low:high] = (keep_ref[m, v].astype(F32) + got_ref[m, v].astype(F32)).astype(out.dtype)
                low = high
        return carry

    lax.fori_loop(0, kept[0].shape[1], one, 0)


def join(kept, received):
    n_own, n_var, held = kept[0].shape[:3]
    side = sum(x.shape[3] for x in kept)
    sent = BF16 if held % 16 == 0 else F32
    vmem = pl.BlockSpec(memory_space=pltpu.VMEM)
    return pl.pallas_call(
        functools.partial(join_kernel, len(kept)),
        out_shape=[jax.ShapeDtypeStruct((n_var, held, side), sent if m else F32) for m in range(n_own)],
        in_specs=[vmem] * (2 * len(kept)),
        out_specs=[vmem] * n_own,
        compiler_params=pltpu.CompilerParams(vmem_limit_bytes=16 * 2**20),
        name="join",
    )(*kept, *received)


def cover_kernel(group, self_ref, prev_ref, scale_ref, diag_out, lower_out, scale, diag, lower, sems):
    count, width = self_ref.shape[:2]
    scale[pl.ds(0, 8), :] = jnp.zeros((8, width), F32)
    scale[pl.ds(8, count), :] = scale_ref[...].astype(F32)
    lower[0] = jnp.zeros((width, width), BF16)

    def copies(g):
        some = pl.ds(g * group, group)
        return (
            pltpu.make_async_copy(diag.at[some], diag_out.at[some], sems.at[0, g]),
            pltpu.make_async_copy(lower.at[some], lower_out.at[some], sems.at[1, g]),
        )

    def turn(g, carry):
        for i in range(group):
            k = g * group + i
            mine, prev, after = self_ref[k], prev_ref[k], prev_ref[jnp.minimum(k + 1, count - 1)]
            here = scale[pl.ds(k + 8, 1), :].astype(BF16)
            back = scale[pl.ds(k + 7, 1), :].astype(BF16)
            left = jnp.concatenate(
                [
                    jnp.concatenate([mine * here, prev * back], axis=1),
                    jnp.concatenate([after * here, jnp.zeros_like(after)], axis=1),
                ],
                axis=0,
            )
            both = lax.dot_general(left, jnp.concatenate([mine, prev], axis=1), NT, preferred_element_type=F32)
            diag[k] = both[:width].astype(BF16)
            lower[k + 1] = both[width:].astype(BF16)
        for copy in copies(g):
            copy.start()
        return carry

    lax.fori_loop(0, count // group, turn, 0)

    def finish(g, carry):
        for copy in copies(g):
            copy.wait()
        return carry

    lax.fori_loop(0, count // group, finish, 0)


def first_kernel(self_ref, prev_ref, scale_ref, got_ref, diag_in, lower_in, diag_out, lower_out, mine, prev, scale, diag, lower, sems):
    width = mine.shape[1]
    held = [
        pltpu.make_async_copy(self_ref.at[pl.ds(0, 1)], mine, sems.at[0]),
        pltpu.make_async_copy(prev_ref.at[pl.ds(0, 1)], prev, sems.at[1]),
        pltpu.make_async_copy(scale_ref.at[pl.ds(0, 16)], scale, sems.at[2]),
    ]
    for copy in held:
        copy.start()
    for copy in held:
        copy.wait()
    here = scale[...].astype(F32)[0:1].astype(BF16)
    back = got_ref[pl.ds(width, 1), :]
    scaled = prev[0] * back
    left = jnp.concatenate([mine[0] * here, scaled], axis=1)
    right = jnp.concatenate([mine[0], prev[0]], axis=1)
    diag[0] = lax.dot_general(left, right, NT, preferred_element_type=F32).astype(BF16)
    lower[0] = lax.dot_general(scaled, got_ref[pl.ds(0, width), :], NT, preferred_element_type=F32).astype(BF16)
    done = [
        pltpu.make_async_copy(diag, diag_out.at[pl.ds(0, 1)], sems.at[3]),
        pltpu.make_async_copy(lower, lower_out.at[pl.ds(0, 1)], sems.at[4]),
    ]
    for copy in done:
        copy.start()
    for copy in done:
        copy.wait()


def cover(cover_self, cover_prev, scaling):
    count, width = cover_self.shape[:2]
    group = 16
    hbm, vmem = pl.BlockSpec(memory_space=pltpu.HBM), pl.BlockSpec(memory_space=pltpu.VMEM)
    return pl.pallas_call(
        functools.partial(cover_kernel, group),
        out_shape=[jax.ShapeDtypeStruct(cover_self.shape, BF16)] * 2,
        in_specs=[vmem] * 3,
        out_specs=[hbm, hbm],
        scratch_shapes=[
            pltpu.VMEM((8 + count, width), F32),
            pltpu.VMEM(cover_self.shape, BF16),
            pltpu.VMEM((count + 1, width, width), BF16),
            pltpu.SemaphoreType.DMA((2, count // group)),
        ],
        compiler_params=pltpu.CompilerParams(vmem_limit_bytes=16 * 2**20),
        cost_estimate=pl.CostEstimate(
            flops=2 * count * width * 4 * width * width, bytes_accessed=4 * 2 * count * width * width, transcendentals=0
        ),
        name="cover",
    )(cover_self, cover_prev, scaling)


def first_cover(cover_self, cover_prev, scaling, got, diag, lower):
    width = cover_self.shape[1]
    hbm, vmem = pl.BlockSpec(memory_space=pltpu.HBM), pl.BlockSpec(memory_space=pltpu.VMEM)
    block = pltpu.VMEM((1, width, width), BF16)
    cover_self, cover_prev, scaling = (pltpu.with_memory_space_constraint(x, pltpu.HBM) for x in (cover_self, cover_prev, scaling))
    return pl.pallas_call(
        first_kernel,
        out_shape=[jax.ShapeDtypeStruct(x.shape, x.dtype) for x in (diag, lower)],
        in_specs=[hbm, hbm, hbm, vmem, hbm, hbm],
        out_specs=[hbm, hbm],
        input_output_aliases={4: 0, 5: 1},
        scratch_shapes=[block, block, pltpu.VMEM((16, width), BF16), block, block, pltpu.SemaphoreType.DMA((5,))],
        name="first_cover",
    )(cover_self, cover_prev, scaling, got, diag, lower)


def body(capacity_blocks, capacity_rows, cover_self, cover_prev, scaling):
    n_var, n_own, n_sub = (lax.axis_size(a) for a in AXES)
    tail = jnp.concatenate([cover_self[-1], scaling[-1:]], axis=0)
    side = CAP * capacity_blocks.shape[2]
    sums = capacity(capacity_blocks, capacity_rows, scaling, side // 4 * 3, ("own", "own"))
    received = [swap(send, "sub", 1) for _, send in sums]
    received, tail, covered = lax.optimization_barrier((received, tail, (cover_self, cover_prev, scaling)))
    total = join([keep for keep, _ in sums], received)
    got = shifted(tail, AXES, 1)
    for axis in ("own", "var"):
        arrived = [swap(total[m].astype(BF16), axis, m) for m in send_order(axis)]
        total = functools.reduce(lambda a, b: a + b.astype(F32), arrived, total[0])
        if axis == "own":
            diag, lower = cover(*covered)
            total, diag, lower, got = lax.optimization_barrier((total, diag, lower, got))
    diag, lower = first_cover(cover_self, cover_prev, scaling, got, diag, lower)
    return (diag, lower, total)


def solution(mesh):
    split = P(AXES)
    return jax.shard_map(
        body, mesh=mesh, in_specs=(split,) * 5, out_specs=(split,) * 3, check_vma=False
    )
```
